32 devices in a mesh: groups: 2 (over x), dp: 4 (over y, core), hidden: 4 (over z).
Axes of the slice: x: 2, y: 2, z: 4, core: 2. Of those that a mesh axis runs over, the one named last changes fastest.
Arguments:
- activations: bfloat16 [24576, 8192], P(('groups', 'dp'), 'hidden'), parts along dimension 0, may hold values from -6 to 6
- cotangent: bfloat16 [24576, 8192], P(('groups', 'dp'), 'hidden'), parts along dimension 0
- up_factor_matrix: bfloat16 [8192, 64], P('hidden'), may hold values from -0.0625 to 0.0625
- input_sketch: bfloat16 [8192, 128], P('hidden'), may hold values from -0.0625 to 0.0625
- rank_sketch: float32 [64, 32], replicated, may hold values from -0.75 to 0.75
Outputs:
- features: bfloat16 [48, 4096], P(('groups', 'dp'), 'hidden'), parts along dimension 0
- scores: float32 [48, 24], P(('groups', 'dp'), 'hidden'), parts along dimension 0
The draws below stay inside these ranges and needn't reach their ends.
There are 2 independent parts, one for each index of `groups`. The reference program is written for one: setup_inputs(seed, part) draws one part's arguments, and reference() takes and returns one part's arrays. A program takes and returns all parts, laid end to end along the dimension named above; an argument that names none is the same for every part. Nothing has to cross between parts.
All inputs are finite; a program needn't handle non-finite values.
Results may differ from the reference program's by a relative error of at most 0.0017.
Values may be sent and summed in bfloat16 or wider, within the bound.
A program may use at most 64 MiB of HBM per device.

```python
import math
import jax
import jax.numpy as jnp
from jax import lax

D_IN = 8192
OUTPUT_WIDTH = 8192
LOW_RANK = 64
K_R = 32
K_IN = 128
FEAT = 4096
SEQ = 512
N_EX = 24


def draw_cotangent(key, part):
    key_ex, key_tok, key_base = jax.random.split(key, 3)
    ex_index = jnp.arange(N_EX, dtype=jnp.float32)
    trend = 3.0 ** (ex_index / max(N_EX - 1, 1))
    example_scale = trend * jnp.exp(jax.random.uniform(key_ex, (N_EX,), minval=-0.5, maxval=0.5))
    tok_scale = jnp.exp(jax.random.uniform(key_tok, (N_EX * SEQ,), minval=0.0, maxval=2.3))
    row_scale = jnp.repeat(example_scale, SEQ) * tok_scale
    base_values = jax.random.normal(key_base, (N_EX * SEQ, OUTPUT_WIDTH))
    return (base_values * row_scale[:, None] * 0.2).astype(jnp.bfloat16)


def level_of(stream_key, dims, shards, smallest, high):
    def one(position, blocks):
        steps = jax.random.uniform(jax.random.fold_in(jax.random.fold_in(stream_key, 6), position), (blocks,), jnp.float32, smallest / len(shards), high / len(shards))
        return jnp.repeat(jnp.exp(steps), dims[position] // blocks).reshape((-1,) + (1,) * (len(dims) - position - 1))

    factor_of = one(*shards[0])
    for cut in shards[1:]:
        factor_of = factor_of * one(*cut)
    return factor_of


def bell_draw(key, extent, deviation, reach, cuts=(), kind=jnp.bfloat16):
    result = deviation * jax.random.normal(key, extent, jnp.float32)
    if cuts:
        result = result * level_of(key, extent, cuts, -0.22, 0.18)
    return jnp.clip(result, -reach, reach).astype(kind)


def setup_inputs(seed: int = 0, part: int = 0) -> dict:
    seeds = jax.random.split(jax.random.key(seed), 6)
    part_keys = jax.random.split(jax.random.fold_in(seeds[5], part), 6)
    return {
        "activations": bell_draw(part_keys[0], (N_EX * SEQ, D_IN), 1.0, 6.0, ((0, 4), (1, 4))),
        "cotangent": draw_cotangent(jax.random.fold_in(jax.random.fold_in(seeds[5], part), 71), part),
        "up_factor_matrix": bell_draw(seeds[2], (OUTPUT_WIDTH, LOW_RANK), OUTPUT_WIDTH ** -0.5, 0.0625, ((0, 4),)),
        "input_sketch": bell_draw(seeds[3], (D_IN, K_IN), D_IN ** -0.5, 0.0625, ((0, 4),)),
        "rank_sketch": bell_draw(seeds[4], (LOW_RANK, K_R), LOW_RANK ** -0.5, 0.75, (), jnp.float32),
    }


epsilon = 1e-05

def reference(activations, cotangent, up_factor_matrix, input_sketch, rank_sketch):
    backward_pass = jnp.dot(cotangent, up_factor_matrix, preferred_element_type=jnp.float32)
    rank_side = jnp.dot(backward_pass, rank_sketch, precision=lax.Precision.HIGHEST)
    input_side = jnp.dot(activations, input_sketch, preferred_element_type=jnp.float32)
    rank_side = rank_side.reshape(N_EX, SEQ, K_R)
    input_side = input_side.reshape(N_EX, SEQ, K_IN)
    outer = jnp.einsum('esa,esb->eab', rank_side, input_side, precision=lax.Precision.HIGHEST)
    features = outer.reshape(N_EX, FEAT).astype(jnp.bfloat16)
    widened = features.astype(jnp.float32)
    weight = 1.0 / (lax.optimization_barrier(jnp.sum(widened * widened, axis=0)) / N_EX + epsilon)
    scores = jnp.dot(widened * weight, widened.T, precision=lax.Precision.HIGHEST) / math.sqrt(FEAT)
    return (features, scores)
```

```python
import functools
import math

import jax
import jax.numpy as jnp
from jax import lax
from jax.experimental import pallas as pl
from jax.experimental.pallas import tpu as pltpu
from jax.sharding import PartitionSpec as P

SEQ = 512
PARTS = 2
AHEAD = 4
GROUP = 2
epsilon = 1e-05
MESH = pl.DeviceIdType.MESH
F32, BF16 = jnp.float32, jnp.bfloat16


def halves(x):
    hi = x.astype(BF16)
    return hi, (x - hi.astype(F32)).astype(BF16)


def kernel(
    n, m, act, cot, upf, sketch, rank, feat_out, score_out,
    cotv, actv, upv, skv, rkv, brv, inp, own, pin, sin, pout, sout,
    fpart, fin, rounded, mine, theirs, everyone, part, parts_in,
    load_sem, p_send, p_recv, s_send, s_recv,
    f_send, f_recv, g_send, g_recv, c_send, c_recv,
):
    h, d = lax.axis_index("hidden"), lax.axis_index("dp")
    count = cotv.shape[0]
    k_r, k_in = rkv.shape[1], skv.shape[1]
    rows = k_r // n
    width = SEQ // PARTS

    barrier = pltpu.get_barrier_semaphore()
    for k in range(1, n):
        pl.semaphore_signal(
            barrier, inc=1, device_id={"hidden": lax.rem(h + k, n)}, device_id_type=MESH)
    for k in range(1, m):
        pl.semaphore_signal(
            barrier, inc=1, device_id={"dp": lax.rem(d + k, m)}, device_id_type=MESH)

    def load(s):
        c = s % count
        big, held = (cot, cotv) if s < count else (act, actv)
        return pltpu.make_async_copy(big.at[pl.ds(c * SEQ, SEQ)], held.at[c], load_sem.at[s])

    load_up = pltpu.make_async_copy(upf, upv, load_sem.at[2 * count])
    load_rank = pltpu.make_async_copy(rank, rkv, load_sem.at[2 * count + 1])
    load_sketch = pltpu.make_async_copy(sketch, skv, load_sem.at[2 * count + 2])
    load_up.start()
    load_rank.start()
    for s in range(AHEAD):
        load(s).start()
    load_sketch.start()

    @pl.when(h == 0)
    def _():
        pin[...] = jnp.zeros_like(pin)

    @pl.when(h == n - 1)
    def _():
        sin[...] = jnp.zeros_like(sin)

    load_rank.wait()
    load_up.wait()
    r1 = rkv[...].astype(BF16)
    rest = rkv[...] - r1.astype(F32)
    r2 = rest.astype(BF16)
    r3 = (rest - r2.astype(F32)).astype(BF16)
    wide = jnp.dot(upv[...], jnp.concatenate([r1, r2, r3], 1), preferred_element_type=F32)
    merged = wide[:, :k_r] + (wide[:, k_r:2 * k_r] + wide[:, 2 * k_r:])
    hi, lo = halves(merged)
    brv[...] = jnp.concatenate([hi, lo], 1)

    def to_right(q, source):
        return pltpu.make_async_remote_copy(
            source.at[q], pin.at[q], p_send.at[q], p_recv.at[q],
            device_id={"hidden": lax.rem(h + 1, n)}, device_id_type=MESH)

    def to_left(q, source):
        return pltpu.make_async_remote_copy(
            source.at[q], sin.at[q], s_send.at[q], s_recv.at[q],
            device_id={"hidden": lax.rem(h + n - 1, n)}, device_id_type=MESH)

    def f_copy(k, g):
        return pltpu.make_async_remote_copy(
            fpart.at[g, lax.rem(h + k, n)], fin.at[k - 1, g],
            f_send.at[k - 1, g], f_recv.at[k - 1, g],
            device_id={"hidden": lax.rem(h + k, n)}, device_id_type=MESH)

    def product(s):
        load(s).wait()
        if s + AHEAD < 2 * count:
            load(s + AHEAD).start()
        c = s % count
        if s < count:
            flat = jnp.dot(cotv[c], brv[...], preferred_element_type=F32).T
            total = flat[:k_r] + flat[k_r:]
            for j in range(PARTS):
                own[c * PARTS + j] = total[:, j * width:(j + 1) * width]
            if s == 0:
                pl.semaphore_wait(barrier, n + m - 2)

            @pl.when(h == 0)
            def _():
                for j in range(PARTS):
                    to_right(c * PARTS + j, own).start()

            @pl.when(h == n - 1)
            def _():
                for j in range(PARTS):
                    to_left(c * PARTS + j, own).start()
        else:
            if s == count:
                load_sketch.wait()
            side = jnp.dot(actv[c], skv[...], preferred_element_type=F32)
            hi, lo = halves(side)
            inp[c] = jnp.concatenate([hi, lo], 1)

    def forward(q, place, right):
        @pl.when(h == place)
        def _():
            if right:
                to_right(q, pout).wait_recv()
                pout[q] = pin[q] + own[q]
                to_right(q, pout).start()
            else:
                to_left(q, sout).wait_recv()
                sout[q] = sin[q] + own[q]
                to_left(q, sout).start()

    def finish(c):
        span = range(c * PARTS, (c + 1) * PARTS)

        @pl.when(h == n - 1)
        def _():
            for q in span:
                to_right(q, pout).wait_recv()

        @pl.when(h == 0)
        def _():
            for q in span:
                to_left(q, sout).wait_recv()

        total = jnp.concatenate([own[q] + (pin[q] + sin[q]) for q in span], 1)
        hi, lo = halves(total)
        out = jnp.dot(jnp.concatenate([hi, lo], 0), inp[c], preferred_element_type=F32)
        block = out[:k_r, :k_in] + (
            (out[:k_r, k_in:] + out[k_r:, :k_in]) + out[k_r:, k_in:])
        g, j = c // GROUP, c % GROUP
        for k in range(n):
            fpart[g, k, j] = block[k * rows:(k + 1) * rows]
        if j == GROUP - 1:
            for k in range(1, n):
                f_copy(k, g).start()

    events = []
    for s in range(2 * count):
        events.append((float(s), 0, functools.partial(product, s)))
    step_link, step_hop = 2.3 / PARTS, 1.5
    for q in range(count * PARTS):
        ready = 1 + q // PARTS

        def arrival(hops):
            first = 1 + hops * (step_link + step_hop) + step_link * q
            return max(first, ready + hops * (step_link + step_hop))

        for place in range(1, n - 1):
            events.append((arrival(place), 1, functools.partial(forward, q, place, True)))
            events.append((arrival(n - 1 - place), 1, functools.partial(forward, q, place, False)))
        if q % PARTS == PARTS - 1:
            c = q // PARTS
            events.append((max(arrival(n - 1), count + c + 1), 2, functools.partial(finish, c)))
    for event in sorted(events, key=lambda e: e[:2]):
        event[2]()

    groups = count // GROUP
    for g in range(groups):
        for k in range(1, n):
            f_copy(k, g).wait_recv()
        for j in range(GROUP):
            value = fpart[g, h, j]
            for k in range(1, n):
                value = value + fin[k - 1, g, j]
            rounded[pl.ds((g * GROUP + j) * rows, rows), :] = value.astype(BF16).astype(F32)

    used = count * rows
    mine[pl.ds(0, used), :] = rounded[...].astype(BF16)

    def g_copy(k):
        return pltpu.make_async_remote_copy(
            mine, theirs.at[k - 1], g_send.at[k - 1], g_recv.at[k - 1],
            device_id={"dp": lax.rem(d + k, m)}, device_id_type=MESH)

    for k in range(1, m):
        g_copy(k).start()
    everyone[pl.ds(pl.multiple_of(d * used, 8), used), :] = rounded[...]
    for a in range(rows):
        feat_out[:, a * k_in:(a + 1) * k_in] = (
            rounded[pl.ds(a, count, stride=rows), :].astype(BF16))
    part[...] = jnp.zeros_like(part)
    for k in range(1, m):
        g_copy(k).wait_recv()
        sender = lax.rem(d + m - k, m)
        everyone[pl.ds(pl.multiple_of(sender * used, 8), used), :] = (
            theirs[k - 1][:used].astype(F32))

    columns, scaled = [], []
    for a in range(rows):
        y = everyone[pl.ds(a, m * count, stride=rows), :]
        squares = jnp.sum(y * y, axis=0, keepdims=True)
        weight = 1.0 / (squares / (m * count) + epsilon)
        columns.append(y.astype(BF16))
        scaled.append(rounded[pl.ds(a, count, stride=rows), :] * weight)
    y = jnp.concatenate(columns, 1)
    hi, lo = halves(jnp.concatenate(scaled, 1))
    across = (((1,), (1,)), ((), ()))
    dots = lax.dot_general(hi, y, across, preferred_element_type=F32) + lax.dot_general(
        lo, y, across, preferred_element_type=F32)
    part[pl.ds(0, count), pl.ds(0, m * count)] = dots / math.sqrt(k_r * k_in)

    def c_copy(k):
        return pltpu.make_async_remote_copy(
            part, parts_in.at[k - 1], c_send.at[k - 1], c_recv.at[k - 1],
            device_id={"hidden": lax.rem(h + k, n)}, device_id_type=MESH)

    for k in range(1, n):
        c_copy(k).start()
    total = part[...]
    for k in range(1, n):
        c_copy(k).wait_recv()
        total = total + parts_in[k - 1]
    cols = score_out.shape[1]
    for place in range(n):
        @pl.when(h == place)
        def _():
            score_out[...] = total[:count, place * cols:(place + 1) * cols]

    @pl.when(h < n - 1)
    def _():
        for q in range(count * PARTS):
            to_right(q, own).wait_send()

    @pl.when(h > 0)
    def _():
        for q in range(count * PARTS):
            to_left(q, own).wait_send()

    for k in range(1, n):
        for g in range(groups):
            f_copy(k, g).wait_send()
        c_copy(k).wait_send()
    for k in range(1, m):
        g_copy(k).wait_send()


def per_device(n, m, activations, cotangent, up_factor_matrix, input_sketch, rank_sketch):
    tokens, depth = activations.shape
    count = tokens // SEQ
    low, k_r = rank_sketch.shape
    k_in = input_sketch.shape[1]
    rows = k_r // n
    used = count * rows
    padded = -(-used // 16) * 16
    lanes = -(-m * count // 128) * 128
    pieces, width = count * PARTS, SEQ // PARTS
    groups = count // GROUP
    vm, dma = pltpu.VMEM, pltpu.SemaphoreType.DMA
    piece = vm((pieces, k_r, width), F32)
    return pl.pallas_call(
        functools.partial(kernel, n, m),
        out_shape=(
            jax.ShapeDtypeStruct((count, rows * k_in), BF16),
            jax.ShapeDtypeStruct((count, m * count // n), F32),
        ),
        in_specs=[pl.BlockSpec(memory_space=pl.ANY)] * 5,
        out_specs=(pl.BlockSpec(memory_space=pltpu.VMEM),) * 2,
        scratch_shapes=[
            vm((count, SEQ, depth), BF16),
            vm((count, SEQ, depth), BF16),
            vm((depth, low), BF16),
            vm((depth, k_in), BF16),
            vm((low, k_r), F32),
            vm((depth, 2 * k_r), BF16),
            vm((count, SEQ, 2 * k_in), BF16),
            piece, piece, piece, piece, piece,
            vm((groups, n, GROUP, rows, k_in), F32),
            vm((n - 1, groups, GROUP, rows, k_in), F32),
            vm((used, k_in), F32),
            vm((padded, k_in), BF16),
            vm((m - 1, padded, k_in), BF16),
            vm((m * used, k_in), F32),
            vm((8, lanes), F32),
            vm((n - 1, 8, lanes), F32),
            dma((2 * count + 3,)),
            dma((pieces,)), dma((pieces,)), dma((pieces,)), dma((pieces,)),
            dma((n - 1, groups)), dma((n - 1, groups)),
            dma((m - 1,)), dma((m - 1,)),
            dma((n - 1,)), dma((n - 1,)),
        ],
        compiler_params=pltpu.CompilerParams(
            collective_id=0, has_side_effects=True, vmem_limit_bytes=52 * 2**20),
        cost_estimate=pl.CostEstimate(
            flops=2 * tokens * depth * (2 * k_r + k_in),
            bytes_accessed=4 * tokens * depth, transcendentals=0),
    )(activations, cotangent, up_factor_matrix, input_sketch, rank_sketch)


def solution(mesh):
    placed = (
        P(("groups", "dp"), "hidden"),
        P(("groups", "dp"), "hidden"),
        P("hidden", None),
        P("hidden", None),
        P(),
    )
    return jax.shard_map(
        functools.partial(per_device, mesh.shape["hidden"], mesh.shape["dp"]),
        mesh=mesh,
        in_specs=placed,
        out_specs=(P(("groups", "dp"), "hidden"), P(("groups", "dp"), "hidden")),
        check_vma=False,
    )
```

```python
import functools
import math

import jax
import jax.numpy as jnp
from jax import lax
from jax.experimental import pallas as pl
from jax.experimental.pallas import tpu as pltpu
from jax.sharding import PartitionSpec as P

SEQ = 512
PARTS = 2
AHEAD = 4
LAG = 3
epsilon = 1e-05
MESH = pl.DeviceIdType.MESH
F32, BF16 = jnp.float32, jnp.bfloat16


def halves(x):
    hi = x.astype(BF16)
    return hi, (x - hi.astype(F32)).astype(BF16)


def kernel(
    n, m, act, cot, upf, sketch, rank, feat_out, score_out,
    cotv, actv, upv, skv, rkv, brv, inp, own, pin, sin, pout, sout,
    fpart, fin, rounded, mine, theirs, everyone, part, parts_in,
    load_sem, p_send, p_recv, s_send, s_recv,
    f_send, f_recv, g_send, g_recv, c_send, c_recv,
):
    h, d = lax.axis_index("hidden"), lax.axis_index("dp")
    count = cotv.shape[0]
    k_r, k_in = rkv.shape[0], skv.shape[1]
    rows = k_r // n
    pieces, width = count * PARTS, SEQ // PARTS

    barrier = pltpu.get_barrier_semaphore()
    for k in range(1, n):
        pl.semaphore_signal(
            barrier, inc=1, device_id={"hidden": lax.rem(h + k, n)}, device_id_type=MESH)
    for k in range(1, m):
        pl.semaphore_signal(
            barrier, inc=1, device_id={"dp": lax.rem(d + k, m)}, device_id_type=MESH)

    def load(big, held, c, base):
        return pltpu.make_async_copy(
            big.at[pl.ds(pl.multiple_of(c * SEQ, SEQ), SEQ)], held.at[c], load_sem.at[base + c])

    def load_cot(c):
        return load(cot, cotv, c, 0)

    def load_act(c):
        return load(act, actv, c, count)

    load_up = pltpu.make_async_copy(upf, upv, load_sem.at[2 * count])
    load_rank = pltpu.make_async_copy(rank, rkv, load_sem.at[2 * count + 1])
    load_sketch = pltpu.make_async_copy(sketch, skv, load_sem.at[2 * count + 2])
    load_rank.start()
    load_up.start()
    for c in range(AHEAD):
        load_cot(c).start()
    load_sketch.start()

    @pl.when(h == 0)
    def _():
        pin[...] = jnp.zeros_like(pin)

    @pl.when(h == n - 1)
    def _():
        sin[...] = jnp.zeros_like(sin)

    load_rank.wait()
    load_up.wait()
    r1 = rkv[...].astype(BF16)
    rest = rkv[...] - r1.astype(F32)
    r2 = rest.astype(BF16)
    r3 = (rest - r2.astype(F32)).astype(BF16)
    wide = jnp.dot(jnp.concatenate([r1, r2, r3], 0), upv[...], preferred_element_type=F32)
    merged = wide[:k_r] + (wide[k_r:2 * k_r] + wide[2 * k_r:])
    top = merged.astype(BF16).astype(F32)
    brv[...] = jnp.concatenate([top, merged - top], 0).T.astype(BF16)

    def to_right(source, q):
        return pltpu.make_async_remote_copy(
            source.at[q], pin.at[q], p_send.at[0], p_recv.at[q],
            device_id={"hidden": lax.rem(h + 1, n)}, device_id_type=MESH)

    def to_left(source, q):
        return pltpu.make_async_remote_copy(
            source.at[q], sin.at[q], s_send.at[0], s_recv.at[q],
            device_id={"hidden": lax.rem(h + n - 1, n)}, device_id_type=MESH)

    def forward(step):
        q = step - LAG * h

        @pl.when((h > 0) & (h < n - 1) & (q >= 0) & (q < pieces))
        def _():
            to_right(pout, q).wait_recv()
            pout[q] = pin[q] + own[q]
            to_right(pout, q).start()

        p = step - LAG * (n - 1 - h)

        @pl.when((h > 0) & (h < n - 1) & (p >= 0) & (p < pieces))
        def _():
            to_left(sout, p).wait_recv()
            sout[p] = sin[p] + own[p]
            to_left(sout, p).start()

    def f_copy(k, c):
        return pltpu.make_async_remote_copy(
            fpart.at[lax.rem(h + k, n), c], fin.at[k - 1, c],
            f_send.at[k - 1], f_recv.at[k - 1],
            device_id={"hidden": lax.rem(h + k, n)}, device_id_type=MESH)

    def f_whole(k):
        return pltpu.make_async_remote_copy(
            fpart.at[lax.rem(h + k, n)], fin.at[k - 1],
            f_send.at[k - 1], f_recv.at[k - 1],
            device_id={"hidden": lax.rem(h + k, n)}, device_id_type=MESH)

    pl.semaphore_wait(barrier, n + m - 2)

    def rank_step(c, carry):
        load_cot(c).wait()

        @pl.when(c + AHEAD < count)
        def _():
            load_cot(c + AHEAD).start()

        @pl.when(c + AHEAD >= count)
        def _():
            load_act(c + AHEAD - count).start()

        flat = jnp.dot(cotv[c], brv[...], preferred_element_type=F32).T
        total = flat[:k_r] + flat[k_r:]
        for j in range(PARTS):
            own[c * PARTS + j] = total[:, j * width:(j + 1) * width]

        @pl.when(h == 0)
        def _():
            for j in range(PARTS):
                to_right(own, c * PARTS + j).start()

        @pl.when(h == n - 1)
        def _():
            for j in range(PARTS):
                to_left(own, c * PARTS + j).start()

        forward(c)
        return carry

    lax.fori_loop(0, count, rank_step, 0)
    load_sketch.wait()

    def input_step(c, carry):
        load_act(c).wait()

        @pl.when(c + AHEAD < count)
        def _():
            load_act(c + AHEAD).start()

        side = jnp.dot(actv[c], skv[...], preferred_element_type=F32)
        hi, lo = halves(side)
        inp[c] = jnp.concatenate([hi, lo], 1)
        forward(count + c)
        return carry

    lax.fori_loop(0, count, input_step, 0)

    def finish(c):
        @pl.when(h == n - 1)
        def _():
            for j in range(PARTS):
                to_right(pout, c * PARTS + j).wait_recv()

        @pl.when(h == 0)
        def _():
            for j in range(PARTS):
                to_left(sout, c * PARTS + j).wait_recv()

        total = jnp.concatenate(
            [own[q] + (pin[q] + sin[q]) for q in [c * PARTS + j for j in range(PARTS)]], 1)
        hi, lo = halves(total)
        out = jnp.dot(jnp.concatenate([hi, lo], 0), inp[c], preferred_element_type=F32)
        block = out[:k_r, :k_in] + (
            (out[:k_r, k_in:] + out[k_r:, :k_in]) + out[k_r:, k_in:])
        for k in range(n):
            fpart[k, c] = block[k * rows:(k + 1) * rows]
        for k in range(1, n):
            f_copy(k, c).start()

    late = max(0, -(-(LAG * (n - 2) + pieces - 2 * count) // PARTS) - count)

    def last_step(t, carry):
        for j in range(PARTS):
            forward(2 * count + PARTS * t + j)
        if late:
            pl.when(t >= late)(lambda: finish(t - late))
        else:
            finish(t)
        return carry

    lax.fori_loop(0, count + late, last_step, 0)

    for k in range(1, n):
        f_whole(k).wait_recv()
    for c in range(count):
        value = fpart[h, c]
        for k in range(1, n):
            value = value + fin[k - 1, c]
        rounded[pl.ds(c * rows, rows), :] = value.astype(BF16).astype(F32)

    used = count * rows
    mine[pl.ds(0, used), :] = rounded[...].astype(BF16)

    def g_copy(k):
        return pltpu.make_async_remote_copy(
            mine, theirs.at[k - 1], g_send.at[k - 1], g_recv.at[k - 1],
            device_id={"dp": lax.rem(d + k, m)}, device_id_type=MESH)

    for k in range(1, m):
        g_copy(k).start()
    everyone[pl.ds(pl.multiple_of(d * used, 8), used), :] = rounded[...]
    for a in range(rows):
        feat_out[:, a * k_in:(a + 1) * k_in] = (
            rounded[pl.ds(a, count, stride=rows), :].astype(BF16))
    part[...] = jnp.zeros_like(part)
    for k in range(1, m):
        g_copy(k).wait_recv()
        sender = lax.rem(d + m - k, m)
        everyone[pl.ds(pl.multiple_of(sender * used, 8), used), :] = (
            theirs[k - 1][:used].astype(F32))

    columns, scaled = [], []
    for a in range(rows):
        y = everyone[pl.ds(a, m * count, stride=rows), :]
        squares = jnp.sum(y * y, axis=0, keepdims=True)
        weight = 1.0 / (squares / (m * count) + epsilon)
        columns.append(y.astype(BF16))
        scaled.append(rounded[pl.ds(a, count, stride=rows), :] * weight)
    y = jnp.concatenate(columns, 1)
    hi, lo = halves(jnp.concatenate(scaled, 1))
    across = (((1,), (1,)), ((), ()))
    dots = lax.dot_general(hi, y, across, preferred_element_type=F32) + lax.dot_general(
        lo, y, across, preferred_element_type=F32)
    part[pl.ds(0, count), pl.ds(0, m * count)] = dots / math.sqrt(k_r * k_in)

    def c_copy(k):
        return pltpu.make_async_remote_copy(
            part, parts_in.at[k - 1], c_send.at[k - 1], c_recv.at[k - 1],
            device_id={"hidden": lax.rem(h + k, n)}, device_id_type=MESH)

    for k in range(1, n):
        c_copy(k).start()
    total = part[...]
    for k in range(1, n):
        c_copy(k).wait_recv()
        total = total + parts_in[k - 1]
    cols = score_out.shape[1]
    for place in range(n):
        @pl.when(h == place)
        def _():
            score_out[...] = total[:count, place * cols:(place + 1) * cols]

    @pl.when(h < n - 1)
    def _():
        pltpu.make_async_remote_copy(
            own, pin, p_send.at[0], p_recv.at[0],
            device_id={"hidden": lax.rem(h + 1, n)}, device_id_type=MESH).wait_send()

    @pl.when(h > 0)
    def _():
        pltpu.make_async_remote_copy(
            own, sin, s_send.at[0], s_recv.at[0],
            device_id={"hidden": lax.rem(h + n - 1, n)}, device_id_type=MESH).wait_send()

    for k in range(1, n):
        f_whole(k).wait_send()
        c_copy(k).wait_send()
    for k in range(1, m):
        g_copy(k).wait_send()


def per_device(n, m, activations, cotangent, up_factor_matrix, input_sketch, rank_sketch):
    tokens, depth = activations.shape
    count = tokens // SEQ
    low, k_r = rank_sketch.shape
    k_in = input_sketch.shape[1]
    rows = k_r // n
    used = count * rows
    padded = -(-used // 16) * 16
    lanes = -(-m * count // 128) * 128
    pieces, width = count * PARTS, SEQ // PARTS
    vm, dma = pltpu.VMEM, pltpu.SemaphoreType.DMA
    piece = vm((pieces, k_r, width), F32)
    return pl.pallas_call(
        functools.partial(kernel, n, m),
        out_shape=(
            jax.ShapeDtypeStruct((count, rows * k_in), BF16),
            jax.ShapeDtypeStruct((count, m * count // n), F32),
        ),
        in_specs=[pl.BlockSpec(memory_space=pltpu.HBM)] * 5,
        out_specs=(pl.BlockSpec(memory_space=pltpu.VMEM),) * 2,
        scratch_shapes=[
            vm((count, SEQ, depth), BF16),
            vm((count, SEQ, depth), BF16),
            vm((low, depth), BF16),
            vm((depth, k_in), BF16),
            vm((k_r, low), F32),
            vm((depth, 2 * k_r), BF16),
            vm((count, SEQ, 2 * k_in), BF16),
            piece, piece, piece, piece, piece,
            vm((n, count, rows, k_in), F32),
            vm((n - 1, count, rows, k_in), F32),
            vm((used, k_in), F32),
            vm((padded, k_in), BF16),
            vm((m - 1, padded, k_in), BF16),
            vm((m * used, k_in), F32),
            vm((8, lanes), F32),
            vm((n - 1, 8, lanes), F32),
            dma((2 * count + 3,)),
            dma((1,)), dma((pieces,)), dma((1,)), dma((pieces,)),
            dma((n - 1,)), dma((n - 1,)),
            dma((m - 1,)), dma((m - 1,)),
            dma((n - 1,)), dma((n - 1,)),
        ],
        compiler_params=pltpu.CompilerParams(
            collective_id=0, has_side_effects=True, vmem_limit_bytes=64 * 2**20),
        cost_estimate=pl.CostEstimate(
            flops=2 * tokens * depth * (2 * k_r + k_in),
            bytes_accessed=4 * tokens * depth, transcendentals=0),
    )(activations, cotangent, up_factor_matrix.T, input_sketch, rank_sketch.T)


def solution(mesh):
    placed = (
        P(("groups", "dp"), "hidden"),
        P(("groups", "dp"), "hidden"),
        P("hidden", None),
        P("hidden", None),
        P(),
    )
    return jax.shard_map(
        functools.partial(per_device, mesh.shape["hidden"], mesh.shape["dp"]),
        mesh=mesh,
        in_specs=placed,
        out_specs=(P(("groups", "dp"), "hidden"), P(("groups", "dp"), "hidden")),
        check_vma=False,
    )
```

```python
import functools
import math

import jax
import jax.numpy as jnp
from jax import lax
from jax.experimental import pallas as pl
from jax.experimental.pallas import tpu as pltpu
from jax.sharding import PartitionSpec as P

SEQ = 512
PARTS = 2
AHEAD = 4
LAG = 2
epsilon = 1e-05
MESH = pl.DeviceIdType.MESH
F32, BF16 = jnp.float32, jnp.bfloat16


def halves(x):
    hi = x.astype(BF16)
    return hi, (x - hi.astype(F32)).astype(BF16)


def kernel(
    n, m, act, cot, upf, sketch, rank, feat_out, score_out,
    cotv, actv, upv, skv, rkv, brv, inp, own, pin, sin, pout, sout,
    fpart, fin, rounded, mine, theirs, everyone, part, parts_in,
    load_sem, p_send, p_recv, s_send, s_recv,
    f_send, f_recv, g_send, g_recv, c_send, c_recv,
):
    h, d = lax.axis_index("hidden"), lax.axis_index("dp")
    count = cotv.shape[0]
    k_r, k_in = rkv.shape[0], skv.shape[1]
    rows = k_r // n
    pieces, width = count * PARTS, SEQ // PARTS

    barrier = pltpu.get_barrier_semaphore()
    for k in range(1, n):
        pl.semaphore_signal(
            barrier, inc=1, device_id={"hidden": lax.rem(h + k, n)}, device_id_type=MESH)
    for k in range(1, m):
        pl.semaphore_signal(
            barrier, inc=1, device_id={"dp": lax.rem(d + k, m)}, device_id_type=MESH)

    def load(big, held, c, base):
        return pltpu.make_async_copy(
            big.at[pl.ds(pl.multiple_of(c * SEQ, SEQ), SEQ)], held.at[c], load_sem.at[base + c])

    def load_cot(c):
        return load(cot, cotv, c, 0)

    def load_act(c):
        return load(act, actv, c, count)

    load_up = pltpu.make_async_copy(upf, upv, load_sem.at[2 * count])
    load_rank = pltpu.make_async_copy(rank, rkv, load_sem.at[2 * count + 1])
    load_sketch = pltpu.make_async_copy(sketch, skv, load_sem.at[2 * count + 2])
    load_rank.start()
    load_up.start()
    for c in range(AHEAD):
        load_cot(c).start()
    load_sketch.start()

    @pl.when(h == 0)
    def _():
        pin[...] = jnp.zeros_like(pin)

    @pl.when(h == n - 1)
    def _():
        sin[...] = jnp.zeros_like(sin)

    load_rank.wait()
    load_up.wait()
    r1 = rkv[...].astype(BF16)
    rest = rkv[...] - r1.astype(F32)
    r2 = rest.astype(BF16)
    r3 = (rest - r2.astype(F32)).astype(BF16)
    wide = jnp.dot(jnp.concatenate([r1, r2, r3], 0), upv[...], preferred_element_type=F32)
    merged = wide[:k_r] + (wide[k_r:2 * k_r] + wide[2 * k_r:])
    top = merged.astype(BF16).astype(F32)
    brv[...] = jnp.concatenate([top, merged - top], 0).T.astype(BF16)

    def to_right(source, q):
        return pltpu.make_async_remote_copy(
            source.at[q], pin.at[q], p_send.at[0], p_recv.at[q],
            device_id={"hidden": lax.rem(h + 1, n)}, device_id_type=MESH)

    def to_left(source, q):
        return pltpu.make_async_remote_copy(
            source.at[q], sin.at[q], s_send.at[0], s_recv.at[q],
            device_id={"hidden": lax.rem(h + n - 1, n)}, device_id_type=MESH)

    def forward(step):
        c = step - LAG * h

        @pl.when((h > 0) & (h < n - 1) & (c >= 0) & (c < count))
        def _():
            for q in [c * PARTS + j for j in range(PARTS)]:
                to_right(pout, q).wait_recv()
                pout[q] = pin[q] + own[q]
                to_right(pout, q).start()

        e = step - LAG * (n - 1 - h)

        @pl.when((h > 0) & (h < n - 1) & (e >= 0) & (e < count))
        def _():
            for q in [e * PARTS + j for j in range(PARTS)]:
                to_left(sout, q).wait_recv()
                sout[q] = sin[q] + own[q]
                to_left(sout, q).start()

    def f_copy(k, c):
        return pltpu.make_async_remote_copy(
            fpart.at[lax.rem(h + k, n), c], fin.at[k - 1, c],
            f_send.at[k - 1], f_recv.at[k - 1],
            device_id={"hidden": lax.rem(h + k, n)}, device_id_type=MESH)

    def f_whole(k):
        return pltpu.make_async_remote_copy(
            fpart.at[lax.rem(h + k, n)], fin.at[k - 1],
            f_send.at[k - 1], f_recv.at[k - 1],
            device_id={"hidden": lax.rem(h + k, n)}, device_id_type=MESH)

    pl.semaphore_wait(barrier, n + m - 2)

    def rank_step(c, carry):
        load_cot(c).wait()

        @pl.when(c + AHEAD < count)
        def _():
            load_cot(c + AHEAD).start()

        @pl.when(c + AHEAD >= count)
        def _():
            load_act(c + AHEAD - count).start()

        flat = jnp.dot(cotv[c], brv[...], preferred_element_type=F32).T
        total = flat[:k_r] + flat[k_r:]
        for j in range(PARTS):
            own[c * PARTS + j] = total[:, j * width:(j + 1) * width]

        @pl.when(h == 0)
        def _():
            for j in range(PARTS):
                to_right(own, c * PARTS + j).start()

        @pl.when(h == n - 1)
        def _():
            for j in range(PARTS):
                to_left(own, c * PARTS + j).start()

        forward(c)
        return carry

    lax.fori_loop(0, count, rank_step, 0)
    load_sketch.wait()

    def finish(c):
        @pl.when(h == n - 1)
        def _():
            for j in range(PARTS):
                to_right(pout, c * PARTS + j).wait_recv()

        @pl.when(h == 0)
        def _():
            for j in range(PARTS):
                to_left(sout, c * PARTS + j).wait_recv()

        total = jnp.concatenate(
            [own[q] + (pin[q] + sin[q]) for q in [c * PARTS + j for j in range(PARTS)]], 1)
        hi, lo = halves(total)
        out = jnp.dot(jnp.concatenate([hi, lo], 0), inp[c], preferred_element_type=F32)
        block = out[:k_r, :k_in] + (
            (out[:k_r, k_in:] + out[k_r:, :k_in]) + out[k_r:, k_in:])
        for k in range(n):
            fpart[k, c] = block[k * rows:(k + 1) * rows]
        for k in range(1, n):
            f_copy(k, c).start()

    first = max(count + 1, LAG * (n - 1) + 1)

    def late_step(step, carry):
        @pl.when(step < 2 * count)
        def _():
            c = step - count
            load_act(c).wait()

            @pl.when(c + AHEAD < count)
            def _():
                load_act(c + AHEAD).start()

            side = jnp.dot(actv[c], skv[...], preferred_element_type=F32)
            hi, lo = halves(side)
            inp[c] = jnp.concatenate([hi, lo], 1)

        forward(step)
        pl.when(step >= first)(lambda: finish(step - first))
        return carry

    lax.fori_loop(count, first + count, late_step, 0)

    for k in range(1, n):
        f_whole(k).wait_recv()
    for c in range(count):
        value = fpart[h, c]
        for k in range(1, n):
            value = value + fin[k - 1, c]
        rounded[pl.ds(c * rows, rows), :] = value.astype(BF16).astype(F32)

    used = count * rows
    mine[pl.ds(0, used), :] = rounded[...].astype(BF16)

    def g_copy(k):
        return pltpu.make_async_remote_copy(
            mine, theirs.at[k - 1], g_send.at[k - 1], g_recv.at[k - 1],
            device_id={"dp": lax.rem(d + k, m)}, device_id_type=MESH)

    for k in range(1, m):
        g_copy(k).start()
    everyone[pl.ds(pl.multiple_of(d * used, 8), used), :] = rounded[...]
    for a in range(rows):
        feat_out[:, a * k_in:(a + 1) * k_in] = (
            rounded[pl.ds(a, count, stride=rows), :].astype(BF16))
    part[...] = jnp.zeros_like(part)
    for k in range(1, m):
        g_copy(k).wait_recv()
        sender = lax.rem(d + m - k, m)
        everyone[pl.ds(pl.multiple_of(sender * used, 8), used), :] = (
            theirs[k - 1][:used].astype(F32))

    columns, scaled = [], []
    for a in range(rows):
        y = everyone[pl.ds(a, m * count, stride=rows), :]
        squares = jnp.sum(y * y, axis=0, keepdims=True)
        weight = 1.0 / (squares / (m * count) + epsilon)
        columns.append(y.astype(BF16))
        scaled.append(rounded[pl.ds(a, count, stride=rows), :] * weight)
    y = jnp.concatenate(columns, 1)
    hi, lo = halves(jnp.concatenate(scaled, 1))
    across = (((1,), (1,)), ((), ()))
    dots = lax.dot_general(hi, y, across, preferred_element_type=F32) + lax.dot_general(
        lo, y, across, preferred_element_type=F32)
    part[pl.ds(0, count), pl.ds(0, m * count)] = dots / math.sqrt(k_r * k_in)

    def c_copy(k):
        return pltpu.make_async_remote_copy(
            part, parts_in.at[k - 1], c_send.at[k - 1], c_recv.at[k - 1],
            device_id={"hidden": lax.rem(h + k, n)}, device_id_type=MESH)

    for k in range(1, n):
        c_copy(k).start()
    total = part[...]
    for k in range(1, n):
        c_copy(k).wait_recv()
        total = total + parts_in[k - 1]
    cols = score_out.shape[1]
    for place in range(n):
        @pl.when(h == place)
        def _():
            score_out[...] = total[:count, place * cols:(place + 1) * cols]

    @pl.when(h < n - 1)
    def _():
        pltpu.make_async_remote_copy(
            own, pin, p_send.at[0], p_recv.at[0],
            device_id={"hidden": lax.rem(h + 1, n)}, device_id_type=MESH).wait_send()

    @pl.when(h > 0)
    def _():
        pltpu.make_async_remote_copy(
            own, sin, s_send.at[0], s_recv.at[0],
            device_id={"hidden": lax.rem(h + n - 1, n)}, device_id_type=MESH).wait_send()

    for k in range(1, n):
        f_whole(k).wait_send()
        c_copy(k).wait_send()
    for k in range(1, m):
        g_copy(k).wait_send()


def per_device(n, m, activations, cotangent, up_factor_matrix, input_sketch, rank_sketch):
    tokens, depth = activations.shape
    count = tokens // SEQ
    low, k_r = rank_sketch.shape
    k_in = input_sketch.shape[1]
    rows = k_r // n
    used = count * rows
    padded = -(-used // 16) * 16
    lanes = -(-m * count // 128) * 128
    pieces, width = count * PARTS, SEQ // PARTS
    vm, dma = pltpu.VMEM, pltpu.SemaphoreType.DMA
    piece = vm((pieces, k_r, width), F32)
    return pl.pallas_call(
        functools.partial(kernel, n, m),
        out_shape=(
            jax.ShapeDtypeStruct((count, rows * k_in), BF16),
            jax.ShapeDtypeStruct((count, m * count // n), F32),
        ),
        in_specs=[pl.BlockSpec(memory_space=pltpu.HBM)] * 5,
        out_specs=(pl.BlockSpec(memory_space=pltpu.VMEM),) * 2,
        scratch_shapes=[
            vm((count, SEQ, depth), BF16),
            vm((count, SEQ, depth), BF16),
            vm((low, depth), BF16),
            vm((depth, k_in), BF16),
            vm((k_r, low), F32),
            vm((depth, 2 * k_r), BF16),
            vm((count, SEQ, 2 * k_in), BF16),
            piece, piece, piece, piece, piece,
            vm((n, count, rows, k_in), F32),
            vm((n - 1, count, rows, k_in), F32),
            vm((used, k_in), F32),
            vm((padded, k_in), BF16),
            vm((m - 1, padded, k_in), BF16),
            vm((m * used, k_in), F32),
            vm((8, lanes), F32),
            vm((n - 1, 8, lanes), F32),
            dma((2 * count + 3,)),
            dma((1,)), dma((pieces,)), dma((1,)), dma((pieces,)),
            dma((n - 1,)), dma((n - 1,)),
            dma((m - 1,)), dma((m - 1,)),
            dma((n - 1,)), dma((n - 1,)),
        ],
        compiler_params=pltpu.CompilerParams(
            collective_id=0, has_side_effects=True, vmem_limit_bytes=64 * 2**20 - 2**17),
        cost_estimate=pl.CostEstimate(
            flops=2 * tokens * depth * (2 * k_r + k_in),
            bytes_accessed=4 * tokens * depth, transcendentals=0),
    )(activations, cotangent, up_factor_matrix.T, input_sketch, rank_sketch.T)


def solution(mesh):
    placed = (
        P(("groups", "dp"), "hidden"),
        P(("groups", "dp"), "hidden"),
        P("hidden", None),
        P("hidden", None),
        P(),
    )
    return jax.shard_map(
        functools.partial(per_device, mesh.shape["hidden"], mesh.shape["dp"]),
        mesh=mesh,
        in_specs=placed,
        out_specs=(P(("groups", "dp"), "hidden"), P(("groups", "dp"), "hidden")),
        check_vma=False,
    )
```

```python
import functools
import math

import jax
import jax.numpy as jnp
from jax import lax
from jax.experimental import pallas as pl
from jax.experimental.pallas import tpu as pltpu
from jax.sharding import PartitionSpec as P

SEQ = 512
PARTS = 2
AHEAD = 4
LAG = 2
epsilon = 1e-05
MESH = pl.DeviceIdType.MESH
F32, BF16 = jnp.float32, jnp.bfloat16


def halves(x):
    hi = x.astype(BF16)
    return hi, (x - hi.astype(F32)).astype(BF16)


def kernel(
    n, m, act, cot, upf, sketch, rank, feat_out, score_out,
    cotv, actv, upv, skv, rkv, brv, inp, own, pin, sin, pout, sout,
    fpart, fin, rounded, mine, theirs, everyone, part, parts_in,
    load_sem, p_send, p_recv, s_send, s_recv,
    f_send, f_recv, g_send, g_recv, c_send, c_recv,
):
    h, d = lax.axis_index("hidden"), lax.axis_index("dp")
    count = cotv.shape[0]
    k_r, k_in = rkv.shape[0], skv.shape[1]
    rows = k_r // n
    pieces, width = count * PARTS, SEQ // PARTS

    barrier = pltpu.get_barrier_semaphore()
    for k in range(1, n):
        pl.semaphore_signal(
            barrier, inc=1, device_id={"hidden": lax.rem(h + k, n)}, device_id_type=MESH)
    for k in range(1, m):
        pl.semaphore_signal(
            barrier, inc=1, device_id={"dp": lax.rem(d + k, m)}, device_id_type=MESH)

    def load(big, held, c, base):
        return pltpu.make_async_copy(
            big.at[pl.ds(pl.multiple_of(c * SEQ, SEQ), SEQ)], held.at[c], load_sem.at[base + c])

    def load_cot(c):
        return load(cot, cotv, c, 0)

    def load_act(c):
        return load(act, actv, c, count)

    load_up = pltpu.make_async_copy(upf, upv, load_sem.at[2 * count])
    load_rank = pltpu.make_async_copy(rank, rkv, load_sem.at[2 * count + 1])
    load_sketch = pltpu.make_async_copy(sketch, skv, load_sem.at[2 * count + 2])
    load_rank.start()
    load_up.start()
    for c in range(AHEAD):
        load_cot(c).start()
    load_sketch.start()

    @pl.when(h == 0)
    def _():
        pin[...] = jnp.zeros_like(pin)

    @pl.when(h == n - 1)
    def _():
        sin[...] = jnp.zeros_like(sin)

    load_rank.wait()
    load_up.wait()
    r1 = rkv[...].astype(BF16)
    rest = rkv[...] - r1.astype(F32)
    r2 = rest.astype(BF16)
    r3 = (rest - r2.astype(F32)).astype(BF16)
    wide = jnp.dot(jnp.concatenate([r1, r2, r3], 0), upv[...], preferred_element_type=F32)
    merged = wide[:k_r] + (wide[k_r:2 * k_r] + wide[2 * k_r:])
    top = merged.astype(BF16).astype(F32)
    brv[...] = jnp.concatenate([top, merged - top], 0).T.astype(BF16)

    def to_right(source, q):
        return pltpu.make_async_remote_copy(
            source.at[q], pin.at[q], p_send.at[0], p_recv.at[q],
            device_id={"hidden": lax.rem(h + 1, n)}, device_id_type=MESH)

    def to_left(source, q):
        return pltpu.make_async_remote_copy(
            source.at[q], sin.at[q], s_send.at[0], s_recv.at[q],
            device_id={"hidden": lax.rem(h + n - 1, n)}, device_id_type=MESH)

    def forward(step):
        c = step - LAG * h

        @pl.when((h > 0) & (h < n - 1) & (c >= 0) & (c < count))
        def _():
            for q in [c * PARTS + j for j in range(PARTS)]:
                to_right(pout, q).wait_recv()
                pout[q] = pin[q] + own[q]
                to_right(pout, q).start()

        e = step - LAG * (n - 1 - h)

        @pl.when((h > 0) & (h < n - 1) & (e >= 0) & (e < count))
        def _():
            for q in [e * PARTS + j for j in range(PARTS)]:
                to_left(sout, q).wait_recv()
                sout[q] = sin[q] + own[q]
                to_left(sout, q).start()

    def f_copy(k, c):
        return pltpu.make_async_remote_copy(
            fpart.at[lax.rem(h + k, n), c], fin.at[k - 1, c],
            f_send.at[k - 1], f_recv.at[k - 1],
            device_id={"hidden": lax.rem(h + k, n)}, device_id_type=MESH)

    def f_whole(k):
        return pltpu.make_async_remote_copy(
            fpart.at[lax.rem(h + k, n)], fin.at[k - 1],
            f_send.at[k - 1], f_recv.at[k - 1],
            device_id={"hidden": lax.rem(h + k, n)}, device_id_type=MESH)

    pl.semaphore_wait(barrier, n + m - 2)

    def rank_step(c, carry):
        load_cot(c).wait()

        @pl.when(c + AHEAD < count)
        def _():
            load_cot(c + AHEAD).start()

        @pl.when(c + AHEAD >= count)
        def _():
            load_act(c + AHEAD - count).start()

        flat = jnp.dot(cotv[c], brv[...], preferred_element_type=F32).T
        total = flat[:k_r] + flat[k_r:]
        for j in range(PARTS):
            own[c * PARTS + j] = total[:, j * width:(j + 1) * width]

        @pl.when(h == 0)
        def _():
            for j in range(PARTS):
                to_right(own, c * PARTS + j).start()

        @pl.when(h == n - 1)
        def _():
            for j in range(PARTS):
                to_left(own, c * PARTS + j).start()

        forward(c)
        return carry

    lax.fori_loop(0, count, rank_step, 0)
    load_sketch.wait()

    def arrived(c):
        @pl.when(h == n - 1)
        def _():
            for j in range(PARTS):
                to_right(pout, c * PARTS + j).wait_recv()

        @pl.when(h == 0)
        def _():
            for j in range(PARTS):
                to_left(sout, c * PARTS + j).wait_recv()

    def outer(c):
        total = jnp.concatenate(
            [own[q] + (pin[q] + sin[q]) for q in [c * PARTS + j for j in range(PARTS)]], 1)
        hi, lo = halves(total)
        out = jnp.dot(jnp.concatenate([hi, lo], 0), inp[c], preferred_element_type=F32)
        block = out[:k_r, :k_in] + (
            (out[:k_r, k_in:] + out[k_r:, :k_in]) + out[k_r:, k_in:])
        for k in range(n):
            fpart[k, c] = block[k * rows:(k + 1) * rows]
        for k in range(1, n):
            f_copy(k, c).start()

    def await_act(c):
        load_act(c).wait()

        @pl.when(c + AHEAD < count)
        def _():
            load_act(c + AHEAD).start()

    def input_side(c):
        side = jnp.dot(actv[c], skv[...], preferred_element_type=F32)
        hi, lo = halves(side)
        inp[c] = jnp.concatenate([hi, lo], 1)

    first = max(count + 1, LAG * (n - 1) + 1)

    def act_step(step, carry):
        await_act(step - count)
        input_side(step - count)
        forward(step)
        return carry

    def both_step(step, carry):
        await_act(step - count)
        forward(step - 1)
        arrived(step - first)
        input_side(step - count)
        outer(step - first)
        return carry

    def outer_step(step, carry):
        forward(step - 1)
        arrived(step - first)
        outer(step - first)
        return carry

    split = min(first, 2 * count)
    lax.fori_loop(count, split - 1, act_step, 0)
    await_act(split - 1 - count)
    input_side(split - 1 - count)
    lax.fori_loop(split, 2 * count, both_step, 0)
    for step in range(2 * count, first):
        forward(step - 1)
    lax.fori_loop(max(first, 2 * count), first + count, outer_step, 0)

    for k in range(1, n):
        f_whole(k).wait_recv()
    for c in range(count):
        value = fpart[h, c]
        for k in range(1, n):
            value = value + fin[k - 1, c]
        rounded[pl.ds(c * rows, rows), :] = value.astype(BF16).astype(F32)

    used = count * rows
    mine[pl.ds(0, used), :] = rounded[...].astype(BF16)

    def g_copy(k):
        return pltpu.make_async_remote_copy(
            mine, theirs.at[k - 1], g_send.at[k - 1], g_recv.at[k - 1],
            device_id={"dp": lax.rem(d + k, m)}, device_id_type=MESH)

    for k in range(1, m):
        g_copy(k).start()
    everyone[pl.ds(pl.multiple_of(d * used, 8), used), :] = rounded[...]
    for a in range(rows):
        feat_out[:, a * k_in:(a + 1) * k_in] = (
            rounded[pl.ds(a, count, stride=rows), :].astype(BF16))
    part[...] = jnp.zeros_like(part)
    for k in range(1, m):
        g_copy(k).wait_recv()
        sender = lax.rem(d + m - k, m)
        everyone[pl.ds(pl.multiple_of(sender * used, 8), used), :] = (
            theirs[k - 1][:used].astype(F32))

    columns, scaled = [], []
    for a in range(rows):
        y = everyone[pl.ds(a, m * count, stride=rows), :]
        squares = jnp.sum(y * y, axis=0, keepdims=True)
        weight = 1.0 / (squares / (m * count) + epsilon)
        columns.append(y.astype(BF16))
        scaled.append(rounded[pl.ds(a, count, stride=rows), :] * weight)
    y = jnp.concatenate(columns, 1)
    hi, lo = halves(jnp.concatenate(scaled, 1))
    across = (((1,), (1,)), ((), ()))
    dots = lax.dot_general(hi, y, across, preferred_element_type=F32) + lax.dot_general(
        lo, y, across, preferred_element_type=F32)
    part[pl.ds(0, count), pl.ds(0, m * count)] = dots / math.sqrt(k_r * k_in)

    def c_copy(k):
        return pltpu.make_async_remote_copy(
            part, parts_in.at[k - 1], c_send.at[k - 1], c_recv.at[k - 1],
            device_id={"hidden": lax.rem(h + k, n)}, device_id_type=MESH)

    for k in range(1, n):
        c_copy(k).start()
    total = part[...]
    for k in range(1, n):
        c_copy(k).wait_recv()
        total = total + parts_in[k - 1]
    cols = score_out.shape[1]
    for place in range(n):
        @pl.when(h == place)
        def _():
            score_out[...] = total[:count, place * cols:(place + 1) * cols]

    @pl.when(h < n - 1)
    def _():
        pltpu.make_async_remote_copy(
            own, pin, p_send.at[0], p_recv.at[0],
            device_id={"hidden": lax.rem(h + 1, n)}, device_id_type=MESH).wait_send()

    @pl.when(h > 0)
    def _():
        pltpu.make_async_remote_copy(
            own, sin, s_send.at[0], s_recv.at[0],
            device_id={"hidden": lax.rem(h + n - 1, n)}, device_id_type=MESH).wait_send()

    for k in range(1, n):
        f_whole(k).wait_send()
        c_copy(k).wait_send()
    for k in range(1, m):
        g_copy(k).wait_send()


def per_device(n, m, activations, cotangent, up_factor_matrix, input_sketch, rank_sketch):
    tokens, depth = activations.shape
    count = tokens // SEQ
    low, k_r = rank_sketch.shape
    k_in = input_sketch.shape[1]
    rows = k_r // n
    used = count * rows
    padded = -(-used // 16) * 16
    lanes = -(-m * count // 128) * 128
    pieces, width = count * PARTS, SEQ // PARTS
    vm, dma = pltpu.VMEM, pltpu.SemaphoreType.DMA
    piece = vm((pieces, k_r, width), F32)
    return pl.pallas_call(
        functools.partial(kernel, n, m),
        out_shape=(
            jax.ShapeDtypeStruct((count, rows * k_in), BF16),
            jax.ShapeDtypeStruct((count, m * count // n), F32),
        ),
        in_specs=[pl.BlockSpec(memory_space=pltpu.HBM)] * 5,
        out_specs=(pl.BlockSpec(memory_space=pltpu.VMEM),) * 2,
        scratch_shapes=[
            vm((count, SEQ, depth), BF16),
            vm((count, SEQ, depth), BF16),
            vm((low, depth), BF16),
            vm((depth, k_in), BF16),
            vm((k_r, low), F32),
            vm((depth, 2 * k_r), BF16),
            vm((count, SEQ, 2 * k_in), BF16),
            piece, piece, piece, piece, piece,
            vm((n, count, rows, k_in), F32),
            vm((n - 1, count, rows, k_in), F32),
            vm((used, k_in), F32),
            vm((padded, k_in), BF16),
            vm((m - 1, padded, k_in), BF16),
            vm((m * used, k_in), F32),
            vm((8, lanes), F32),
            vm((n - 1, 8, lanes), F32),
            dma((2 * count + 3,)),
            dma((1,)), dma((pieces,)), dma((1,)), dma((pieces,)),
            dma((n - 1,)), dma((n - 1,)),
            dma((m - 1,)), dma((m - 1,)),
            dma((n - 1,)), dma((n - 1,)),
        ],
        compiler_params=pltpu.CompilerParams(
            collective_id=0, has_side_effects=True, vmem_limit_bytes=64 * 2**20 - 2**17),
        cost_estimate=pl.CostEstimate(
            flops=2 * tokens * depth * (2 * k_r + k_in),
            bytes_accessed=4 * tokens * depth, transcendentals=0),
    )(activations, cotangent, up_factor_matrix.T, input_sketch, rank_sketch.T)


def solution(mesh):
    placed = (
        P(("groups", "dp"), "hidden"),
        P(("groups", "dp"), "hidden"),
        P("hidden", None),
        P("hidden", None),
        P(),
    )
    return jax.shard_map(
        functools.partial(per_device, mesh.shape["hidden"], mesh.shape["dp"]),
        mesh=mesh,
        in_specs=placed,
        out_specs=(P(("groups", "dp"), "hidden"), P(("groups", "dp"), "hidden")),
        check_vma=False,
    )
```
